256 devices in a mesh: blk: 64 (over x_lo, z, y), rep: 4 (over x_hi, core).
Axes of the slice: x: 4 (x_hi: 2, x_lo: 2; x = x_hi * 2 + x_lo), y: 4, z: 8, core: 2. Of those that a mesh axis runs over, the one named last changes fastest.
Arguments:
- image_emb: bfloat16 [65536, 1024], P(('blk', 'rep')), may hold values from -640 to 640
- text_emb: bfloat16 [65536, 1024], P('blk'), may hold values from -9 to 9
- logit_scale: float32 [1], replicated, may hold values from 0.04 to 0.08
Outputs:
- grad_image: float32 [65536, 1024], P(('blk', 'rep'))
- grad_text: float32 [65536, 1024], P(('blk', 'rep'))
- loss: float32 [1], replicated
The draws below stay inside these ranges and needn't reach their ends.
All inputs are finite; a program needn't handle non-finite values.
Results may differ from the reference program's by a relative error of at most 0.002.
Values may be sent and summed in bfloat16 or wider, within the bound.
No kernel may reach another device: no remote copies, remote signals or barrier semaphores. Data moves between devices by JAX's collectives and lax.ppermute only.
A program may use at most 64 MiB of HBM per device.

```python
import math
import jax
import jax.numpy as jnp
from jax import lax

D = 1024
STEPS = 4
BLOCK = 1024
BLOCKS = 64
PAIRS = 65536


def shared_parts(key, tie):
    base = jnp.clip(jax.random.normal(jax.random.fold_in(key, 11), (PAIRS, D), jnp.float32), -4.0, 4.0)
    chosen = jax.random.bernoulli(jax.random.fold_in(key, 12), 1.0 / 64.0, (PAIRS,))
    caption_scale = jnp.exp(jax.random.uniform(jax.random.fold_in(key, 13), (PAIRS,), jnp.float32, math.log(0.5), math.log(2.0)))
    nudge = 0.1 * jnp.clip(jax.random.normal(jax.random.fold_in(key, 14), (PAIRS, D), jnp.float32), -4.0, 4.0)
    follower = jnp.roll(chosen, 1).astype(jnp.float32) * tie
    base = jnp.where(follower[:, None] > 0.5, jnp.roll(base, 1, axis=0) + nudge, base)
    caption_scale = jnp.where(follower > 0.5, jnp.roll(caption_scale, 1), caption_scale)
    return (base, caption_scale, chosen)


def draw_text_emb(key, part):
    tie = 0.0
    base, caption_scale, chosen = shared_parts(key, tie)
    return (caption_scale[:, None] * base).astype(jnp.bfloat16)


def draw_image_emb(key, part):
    tie = 0.0
    widest = 3.0
    base, caption_scale, chosen = shared_parts(key, tie)
    key = jax.random.fold_in(key, 4)
    noise = jnp.clip(jax.random.normal(jax.random.fold_in(key, 1), (PAIRS, D), jnp.float32), -4.0, 4.0)
    row_scale = jnp.exp(jax.random.uniform(jax.random.fold_in(key, 2), (PAIRS,), jnp.float32, math.log(0.3), math.log(widest)))
    strength = jnp.exp(jax.random.uniform(jax.random.fold_in(key, 5), (PAIRS,), jnp.float32, 0.0, math.log(2.0))) * (5000.0 / D)
    mixed = row_scale[:, None] * (0.15 * base + noise)
    aligned = strength[:, None] * base
    picked = chosen.astype(jnp.float32)
    return jnp.where(picked[:, None] > 0.5, aligned, mixed).astype(jnp.bfloat16)


def setup_inputs(seed: int = 0) -> dict:
    keys = jax.random.split(jax.random.key(seed), 4)
    image_emb = draw_image_emb(jax.random.fold_in(keys[3], 71), 0)
    text_emb = draw_text_emb(jax.random.fold_in(keys[3], 71), 0)
    logit_scale = jnp.clip(jax.random.uniform(keys[2], (1,), jnp.float32, 0.04, 0.08), 0.04, 0.08)
    return {"image_emb": image_emb, "text_emb": text_emb, "logit_scale": logit_scale}


def pair_logits(images, captions, multiplier):
    product = lax.dot_general(images, captions, (((1,), (1,)), ((), ())), preferred_element_type=jnp.float32)
    return multiplier * product


def reduce_stats(logits, along):
    highest = jnp.max(logits, axis=along)
    summed = jnp.sum(jnp.exp(logits - jnp.expand_dims(highest, along)), axis=along)
    return highest, summed


def reference(image_emb, text_emb, logit_scale):
    multiplier = logit_scale[0]
    image_blocks = image_emb.reshape(BLOCKS, BLOCK, D)
    text_blocks = text_emb.reshape(BLOCKS, BLOCK, D)

    def make_tile(index, offset):
        images = lax.dynamic_index_in_dim(image_blocks, index, 0, keepdims=False)
        partner = ((index - offset) % BLOCKS).astype(jnp.int32)
        captions = lax.dynamic_index_in_dim(text_blocks, partner, 0, keepdims=False)
        return images, captions, partner, pair_logits(images, captions, multiplier)

    def first_pass(index):
        tiles = [make_tile(index, offset)[3] for offset in range(STEPS)]
        highest, summed = reduce_stats(jnp.concatenate(tiles, axis=1), 1)
        column_parts = [reduce_stats(logits, 0) for logits in tiles]
        high_stack = jnp.stack([part[0] for part in column_parts])
        sum_stack = jnp.stack([part[1] for part in column_parts])
        return highest + jnp.log(summed), high_stack, sum_stack

    indices = jnp.arange(BLOCKS, dtype=jnp.int32)
    row_lse, column_high, column_sums = lax.map(first_pass, indices)
    shifted_high = jnp.stack([jnp.roll(column_high[:, offset], -offset, axis=0) for offset in range(STEPS)])
    shifted_sums = jnp.stack([jnp.roll(column_sums[:, offset], -offset, axis=0) for offset in range(STEPS)])
    column_top = jnp.max(shifted_high, axis=0)
    column_total = jnp.sum(shifted_sums * jnp.exp(shifted_high - column_top[None]), axis=0)
    column_lse = column_top + jnp.log(column_total)
    matched = multiplier * jnp.einsum("nd,nd->n", image_emb.astype(jnp.float32), text_emb.astype(jnp.float32))
    loss_value = (jnp.sum(row_lse) + jnp.sum(column_lse) - 2.0 * jnp.sum(matched)) / (2.0 * PAIRS)
    identity = jnp.eye(BLOCK, dtype=jnp.float32)

    def second_pass(text_grads, index):
        row_now = lax.dynamic_index_in_dim(row_lse, index, 0, keepdims=False)
        image_grad = jnp.zeros((BLOCK, D), jnp.float32)
        for offset in range(STEPS):
            images, captions, partner, logits = make_tile(index, offset)
            column_now = lax.dynamic_index_in_dim(column_lse, partner, 0, keepdims=False)
            averaged = 0.5 * (jnp.exp(logits - row_now[:, None]) + jnp.exp(logits - column_now[None, :]))
            if offset == 0:
                averaged = averaged - identity
            weights = averaged.astype(jnp.bfloat16)
            image_grad = image_grad + multiplier * jnp.dot(weights, captions, preferred_element_type=jnp.float32)
            text_term = multiplier * lax.dot_general(weights, images, (((0,), (0,)), ((), ())), preferred_element_type=jnp.float32)
            current = lax.dynamic_index_in_dim(text_grads, partner, 0, keepdims=False)
            text_grads = lax.dynamic_update_index_in_dim(text_grads, current + text_term, partner, 0)
        return text_grads, image_grad

    text_grads, image_grads = lax.scan(second_pass, jnp.zeros((BLOCKS, BLOCK, D), jnp.float32), indices)
    return image_grads.reshape(PAIRS, D), text_grads.reshape(PAIRS, D), jnp.reshape(loss_value, (1,))
```

```python
import math

import jax
import jax.numpy as jnp
from jax import lax
from jax.experimental import pallas as pl
from jax.experimental.pallas import tpu as pltpu
from jax.sharding import PartitionSpec as P

LOG2E = math.log2(math.e)
LN2 = math.log(2.0)
ORDER = (0, 2, 1, 3)
PLACE = (0, 2, 1, 3)
NT = (((1,), (1,)), ((), ()))
TN = (((0,), (0,)), ((), ()))
F32 = jnp.float32
BF16 = jnp.bfloat16
LIMIT = 48 * 1024 * 1024


def params(**kw):
    return pltpu.CompilerParams(vmem_limit_bytes=LIMIT, **kw)


def stats_of(s, k, col_ref, row_ref, m_scr, l_scr):
    top = jnp.max(s, axis=0, keepdims=True)
    col_ref[...] = top + jnp.log2(jnp.sum(jnp.exp2(s - top), axis=0, keepdims=True))

    @pl.when(k == 0)
    def _():
        m_scr[...] = jnp.full_like(m_scr, -jnp.inf)
        l_scr[...] = jnp.zeros_like(l_scr)

    before = m_scr[...]
    m = jnp.maximum(before, jnp.max(s, axis=1, keepdims=True))
    part = jnp.sum(jnp.exp2(s - m[:, :1]), axis=1, keepdims=True)
    total = l_scr[...] * jnp.exp2(before - m) + part
    m_scr[...] = m
    l_scr[...] = total

    @pl.when(k == 3)
    def _():
        row_ref[...] = jnp.transpose(m + jnp.log2(total))[:1, :]


def own_logits_kernel(order, scale, a, x, t, s_ref, row_ref, col_ref, diag_ref, m_scr, l_scr):
    k = pl.program_id(0)
    mult = scale[0] * LOG2E
    rows = a.shape[0]
    s_ref[:rows, :] = mult * lax.dot_general(a[...], t[...], NT, preferred_element_type=F32)
    s_ref[rows:, :] = mult * lax.dot_general(x[...], t[...], NT, preferred_element_type=F32)
    s = s_ref[...]

    @pl.when(k == 0)
    def _():
        sub = s[:rows, :]
        eye = lax.broadcasted_iota(jnp.int32, sub.shape, 0) == lax.broadcasted_iota(jnp.int32, sub.shape, 1)
        diag_ref[...] = jnp.sum(jnp.where(eye, sub, 0.0), axis=0, keepdims=True)

    stats_of(s, k, col_ref, row_ref, m_scr, l_scr)


def far_logits_kernel(even, scale, a, y, x, v0, v1, s_ref, row_ref, col_ref, m_scr, l_scr):
    k = pl.program_id(0)
    mult = scale[0] * LOG2E
    rows = a.shape[0]

    def run(img, v):
        return mult * lax.dot_general(img, v, NT, preferred_element_type=F32)

    ysel = jnp.where(even[0] == 1, y[...], a[...])
    v = jnp.where(k < 2, v0[...], v1[...])
    s_ref[:rows, :] = run(ysel, v)
    s_ref[rows:, :] = run(x[...], v)
    stats_of(s_ref[...], k, col_ref, row_ref, m_scr, l_scr)


def column(vec):
    return jnp.transpose(jnp.broadcast_to(vec, (128, vec.shape[1])))[:, :1]


def far_text_kernel(even, scale, a, y, x, s, row, col, w_ref, g23, g01, r_scr):
    k = pl.program_id(0)
    rows = a.shape[0]

    @pl.when(k == 0)
    def _():
        r_scr[...] = jnp.transpose(jnp.broadcast_to(row[...], (128, row.shape[1])))

    logits = s[...]
    w = (0.5 * (jnp.exp2(logits - r_scr[:, :1]) + jnp.exp2(logits - col[...]))).astype(BF16)
    w_ref[...] = w
    ysel = jnp.where(even[0] == 1, y[...], a[...])
    g = lax.dot_general(w[:rows], ysel, TN, preferred_element_type=F32)
    g = scale[0] * (g + lax.dot_general(w[rows:], x[...], TN, preferred_element_type=F32))

    @pl.when(k < 2)
    def _():
        g23[...] = g.astype(BF16)

    @pl.when(k >= 2)
    def _():
        g01[...] = g


def rest_kernel(order, scale, a, x, t, s, row, col, wv, v0, v1, g23, g01, gi_ref, gx_ref, gy_ref,
                r_scr, acc_i, acc_x, acc_y):
    k = pl.program_id(0)
    rows = a.shape[0]

    @pl.when(k == 0)
    def _():
        r_scr[...] = jnp.transpose(jnp.broadcast_to(row[...], (128, row.shape[1])))
        acc_i[...] = jnp.zeros_like(acc_i)
        acc_x[...] = jnp.zeros_like(acc_x)
        acc_y[...] = jnp.zeros_like(acc_y)

    logits = s[...]
    avg = 0.5 * (jnp.exp2(logits - r_scr[:, :1]) + jnp.exp2(logits - col[...]))
    ri = lax.broadcasted_iota(jnp.int32, avg.shape, 0)
    ci = lax.broadcasted_iota(jnp.int32, avg.shape, 1)
    avg = avg - jnp.where((ri == ci) & (k == 2), 1.0, 0.0)
    w = avg.astype(BF16)
    g = lax.dot_general(w[:rows], a[...], TN, preferred_element_type=F32)
    g = scale[0] * (g + lax.dot_general(w[rows:], x[...], TN, preferred_element_type=F32))

    @pl.when(k < 2)
    def _():
        g23[...] = g.astype(BF16)

    @pl.when(k >= 2)
    def _():
        g01[...] = g

    v = jnp.where(k >= 2, v0[...], v1[...])
    far = wv[...]
    acc_i[...] += jnp.dot(w[:rows], t[...], preferred_element_type=F32)
    acc_y[...] += jnp.dot(far[:rows], v, preferred_element_type=F32)
    acc_x[...] += (jnp.dot(w[rows:], t[...], preferred_element_type=F32)
                   + jnp.dot(far[rows:], v, preferred_element_type=F32))

    @pl.when(k == 3)
    def _():
        gi_ref[...] = scale[0] * acc_i[...]
        gx_ref[...] = (scale[0] * acc_x[...]).astype(BF16)
        gy_ref[...] = scale[0] * acc_y[...]


def whole(shape):
    return pl.BlockSpec(shape, lambda k, *_: (0,) * len(shape))


def lse2(*parts):
    top = parts[0]
    for p in parts[1:]:
        top = jnp.maximum(top, p)
    total = sum(jnp.exp2(p - top) for p in parts)
    return top + jnp.log2(total)


def per_device(image_emb, text_emb, logit_scale):
    rows, d = image_emb.shape
    blocks = lax.axis_size("blk")
    blk = lax.axis_index("blk")
    rep = lax.axis_index("rep")
    even = blk % 2 == 0
    evens = even.astype(jnp.int32).reshape(1)
    order = jnp.stack([rep ^ m for m in ORDER]).astype(jnp.int32)
    x_route = [(i, (i - 1) % blocks if i % 2 == 0 else (i - 3) % blocks) for i in range(blocks)]
    y_route = [(i, (i - 4) % blocks) for i in range(0, blocks, 2)]
    v_route = [(i, i ^ 1) for i in range(blocks)]
    x_back = [(b, a) for a, b in x_route]
    y_back = [(b, a) for a, b in y_route]

    def hop(value, route):
        return lax.ppermute(value, "blk", route)

    def swap(value, mask):
        return lax.ppermute(value, "rep", [(i, i ^ mask) for i in range(4)])

    first = lax.dynamic_slice_in_dim(text_emb, (rep) * rows, rows, 0)
    second = lax.dynamic_slice_in_dim(text_emb, (rep ^ 2) * rows, rows, 0)
    v0 = hop(jnp.concatenate([first, second]), v_route)
    x = hop(image_emb, x_route)
    y = hop(image_emb, y_route)
    v1 = swap(v0, 1)

    smem = pl.BlockSpec(memory_space=pltpu.SMEM)
    image_spec = whole((rows, d))
    vec = jax.ShapeDtypeStruct
    logits_shape = vec((2 * rows, 4 * rows), F32)
    stat_scratch = [pltpu.VMEM((2 * rows, 128), F32)] * 2
    tile = pl.BlockSpec((2 * rows, rows), lambda k, *_: (0, k))
    lane = pl.BlockSpec((1, rows), lambda k, *_: (0, k))
    logits_cost = pl.CostEstimate(flops=2 * 2 * rows * 4 * rows * d, bytes_accessed=6 << 20, transcendentals=4 << 20)
    s_t, row_t, col_t, diag = pl.pallas_call(
        own_logits_kernel,
        grid_spec=pltpu.PrefetchScalarGridSpec(
            num_scalar_prefetch=1,
            grid=(4,),
            in_specs=[smem, image_spec, image_spec, pl.BlockSpec((rows, d), lambda k, o: (o[k], 0))],
            out_specs=[tile, whole((1, 2 * rows)), lane, whole((1, rows))],
            scratch_shapes=stat_scratch,
        ),
        out_shape=[logits_shape, vec((1, 2 * rows), F32), vec((1, 4 * rows), F32), vec((1, rows), F32)],
        compiler_params=params(),
        cost_estimate=logits_cost,
        name="own_logits",
    )(order, logit_scale, image_emb, x, text_emb)
    s_v, row_v, col_v = pl.pallas_call(
        far_logits_kernel,
        grid=(4,),
        in_specs=[smem, smem, image_spec, image_spec, image_spec,
                  pl.BlockSpec((rows, d), lambda k: (jnp.minimum(k, 1), 0)),
                  pl.BlockSpec((rows, d), lambda k: (jnp.maximum(k - 2, 0), 0))],
        out_specs=[tile, whole((1, 2 * rows)), lane],
        scratch_shapes=stat_scratch,
        out_shape=[logits_shape, vec((1, 2 * rows), F32), vec((1, 4 * rows), F32)],
        compiler_params=params(),
        cost_estimate=logits_cost,
        name="far_logits",
    )(evens, logit_scale, image_emb, y, x, v0, v1)

    r_i, r_xt = row_t[:, :rows], row_t[:, rows:]
    r_y, r_xv = row_v[:, :rows], row_v[:, rows:]
    r_x = lse2(r_xt, r_xv)
    h_i = jnp.where(even, r_i, lse2(r_i, r_y))
    down = hop(jnp.concatenate([h_i, r_x], 1), x_route)
    up = hop(jnp.concatenate([r_x, r_y], 1), x_back)
    h_y = hop(r_i, y_route)
    y_i = hop(r_y, y_back)
    h_x, x_y = down[:, :rows], down[:, rows:]
    x_i, y_x = up[:, :rows], up[:, rows:]
    row_i = jnp.where(even, lse2(r_i, x_i, y_i), lse2(h_i, x_i))
    row_x = jnp.where(even, lse2(h_x, r_x), lse2(h_x, r_x, y_x))
    row_y = jnp.where(even, lse2(r_y, h_y, x_y), row_i)

    both = jnp.concatenate([col_t, col_v])
    quarters = [both[:, q * rows:(q + 1) * rows] for q in range(4)]
    parts = [both]
    for mask in (1, 2, 3):
        got = swap(both, mask)
        parts.append(jnp.concatenate(
            [got[:, q * rows:(q + 1) * rows] for q in (PLACE[ORDER[k] ^ mask] for k in range(4))], 1))
    group = lse2(*parts)
    other = hop(group, v_route)
    cols = lse2(group, other[::-1])
    c_t, c_v = cols[:1], cols[1:]

    late = pl.BlockSpec((2 * rows, rows), lambda k, *_: (0, (k + 2) % 4))
    late_lane = pl.BlockSpec((1, rows), lambda k, *_: (0, (k + 2) % 4))
    early_out = pl.BlockSpec((rows, d), lambda k, *_: (jnp.minimum(k, 1), 0))
    late_out = pl.BlockSpec((rows, d), lambda k, *_: (jnp.maximum(k - 2, 0), 0))
    row_spec = whole((1, 2 * rows))
    w_v, gv23, gv01 = pl.pallas_call(
        far_text_kernel,
        grid=(4,),
        in_specs=[smem, smem, image_spec, image_spec, image_spec, late, row_spec, late_lane],
        out_specs=[late, early_out, late_out],
        out_shape=[vec((2 * rows, 4 * rows), BF16), vec((2 * rows, d), BF16), vec((2 * rows, d), F32)],
        scratch_shapes=[pltpu.VMEM((2 * rows, 128), F32)],
        compiler_params=params(),
        cost_estimate=logits_cost,
        name="far_text",
    )(evens, logit_scale, image_emb, y, x, s_v, jnp.concatenate([row_y, row_x], 1), c_v)
    v_core = swap(gv23, 1)
    gt23, gt01, g_i, g_x, g_y = pl.pallas_call(
        rest_kernel,
        grid_spec=pltpu.PrefetchScalarGridSpec(
            num_scalar_prefetch=1,
            grid=(4,),
            in_specs=[smem, image_spec, image_spec,
                      pl.BlockSpec((rows, d), lambda k, o: (o[(k + 2) % 4], 0)),
                      late, row_spec, late_lane, late,
                      pl.BlockSpec((rows, d), lambda k, *_: (jnp.maximum(k - 2, 0), 0)),
                      pl.BlockSpec((rows, d), lambda k, *_: (jnp.minimum(k, 1), 0))],
            out_specs=[early_out, late_out, image_spec, image_spec, image_spec],
            scratch_shapes=[pltpu.VMEM((2 * rows, 128), F32)] + [pltpu.VMEM((rows, d), F32)] * 3,
        ),
        out_shape=[vec((2 * rows, d), BF16), vec((2 * rows, d), F32), vec((rows, d), F32), vec((rows, d), BF16),
                   vec((rows, d), F32)],
        compiler_params=params(),
        cost_estimate=pl.CostEstimate(flops=3 * 2 * 2 * rows * 4 * rows * d, bytes_accessed=12 << 20,
                                      transcendentals=2 << 20),
        name="rest",
    )(order, logit_scale, image_emb, x, text_emb, s_t, jnp.concatenate([row_i, row_x], 1), c_t, w_v, v0, v1)

    t_core = swap(gt23, 1)
    v_one = (gv01[rows:] + v_core[rows:].astype(F32)).astype(BF16)
    v_zero = (gv01[:rows] + v_core[:rows].astype(F32)).astype(BF16)
    home_one = hop(v_one, v_route)
    x_got = hop(g_x, x_back)
    y_got = hop(g_y.astype(BF16), y_back)
    home_zero = hop(v_zero, v_route)
    one = gt01[rows:] + t_core[rows:].astype(F32) + home_one.astype(F32)
    across = swap(one.astype(BF16), 2)
    grad_text = (gt01[:rows] + t_core[:rows].astype(F32)) + home_zero.astype(F32) + across.astype(F32)
    grad_image = g_i + x_got.astype(F32) + jnp.where(even, y_got.astype(F32), g_y)

    local = LN2 * (jnp.sum(row_i) + jnp.sum(c_t[:, :rows]) - 2.0 * jnp.sum(diag))
    total = jnp.broadcast_to(local, (1, 128))
    step = 1
    while step < blocks:
        total = total + hop(total, [(i, i ^ step) for i in range(blocks)])
        step *= 2
    for mask in (1, 2):
        total = total + swap(total, mask)
    pairs = rows * blocks * 4
    loss = total[0, :1] / (2.0 * pairs)
    return grad_image, grad_text, loss


def solution(mesh):
    placed = (P(("blk", "rep"), None), P("blk", None), P())
    return jax.shard_map(
        per_device,
        mesh=mesh,
        in_specs=placed,
        out_specs=(P(("blk", "rep"), None), P(("blk", "rep"), None), P()),
        check_vma=False,
    )
```

```python
import math

import jax
import jax.numpy as jnp
from jax import lax
from jax.experimental import pallas as pl
from jax.experimental.pallas import tpu as pltpu
from jax.sharding import PartitionSpec as P

LOG2E = math.log2(math.e)
LN2 = math.log(2.0)
ORDER = (0, 2, 1, 3)
PLACE = (0, 2, 1, 3)
NT = (((1,), (1,)), ((), ()))
TN = (((0,), (0,)), ((), ()))
F32 = jnp.float32
BF16 = jnp.bfloat16
CORE = jnp.bfloat16
CORE_V = jnp.float32
LANES = 128
VMEM = pl.BlockSpec(memory_space=pltpu.VMEM)
SMEM = pl.BlockSpec(memory_space=pltpu.SMEM)


ANY = pl.BlockSpec(memory_space=pl.ANY)
HBM = pl.BlockSpec(memory_space=pltpu.HBM)


def local_call(kernel, name, specs, shapes, flops, scratch=(), out_specs=None):
    return pl.pallas_call(
        kernel,
        in_specs=specs,
        out_specs=out_specs or [VMEM] * len(shapes),
        out_shape=[jax.ShapeDtypeStruct(*s) for s in shapes],
        scratch_shapes=list(scratch),
        compiler_params=pltpu.CompilerParams(vmem_limit_bytes=16 * 1024 * 1024),
        cost_estimate=pl.CostEstimate(flops=1, bytes_accessed=1, transcendentals=0),
        name=name,
    )


def fetch(sources, targets, sems):
    copies = [pltpu.make_async_copy(s, t, sems.at[i]) for i, (s, t) in enumerate(zip(sources, targets))]
    for copy in copies:
        copy.start()
    return copies


def fetch_y(even, a, y, target, sem):
    @pl.when(even[0] == 1)
    def _():
        pltpu.make_async_copy(y, target, sem).start()

    @pl.when(even[0] != 1)
    def _():
        pltpu.make_async_copy(a, target, sem).start()

    return pltpu.make_async_copy(y, target, sem)


def columns_of(s):
    top = jnp.max(s, axis=0, keepdims=True)
    return top + jnp.log2(jnp.sum(jnp.exp2(s - top), axis=0, keepdims=True))


def rows_of(s_ref, before):
    slabs = range(0, s_ref.shape[1], LANES)
    m = s_ref[:, :LANES]
    for o in slabs[1:]:
        m = jnp.maximum(m, s_ref[:, o:o + LANES])
    top = jnp.max(m, axis=1, keepdims=True)
    if before is not None:
        top = jnp.maximum(top, before)
    else:
        top = jnp.broadcast_to(top, m.shape)
    part = jnp.exp2(s_ref[:, :LANES] - top)
    for o in slabs[1:]:
        part = part + jnp.exp2(s_ref[:, o:o + LANES] - top)
    total = jnp.sum(part, axis=1, keepdims=True)
    if before is not None:
        total = total + jnp.exp2(before - top)
    return jnp.transpose(top + jnp.log2(total))[:1, :]


def spread(vec):
    return jnp.transpose(jnp.broadcast_to(vec, (LANES, vec.shape[1])))


def quarter(order, t, k, rows):
    return t.at[pl.ds(pl.multiple_of(order[k] * rows, rows), rows), :]


def halves(ref, rows):
    return [ref.at[k * rows:(k + 1) * rows, :] for k in range(2)]


def slice_kernel(order, t, half):
    half[...] = t[...]


def own_image_kernel(order, scale, a_in, t_in, s_out, row_ref, col_ref, diag_ref, a, t, s_ref, sems, out_sems):
    rows = a.shape[0]
    copies = fetch([a_in] + [quarter(order, t_in, k, rows) for k in range(4)], [a] + [t.at[k] for k in range(4)], sems)
    mult = scale[0] * LOG2E
    copies[0].wait()
    stores = []
    for k in range(4):
        copies[1 + k].wait()
        cols = slice(k * rows, (k + 1) * rows)
        s_ref[:, cols] = mult * lax.dot_general(a[...], t[k], NT, preferred_element_type=F32)
        stores.append(pltpu.make_async_copy(s_ref.at[:, cols], s_out.at[:, cols], out_sems.at[k]))
        stores[-1].start()
        col_ref[:, cols] = columns_of(s_ref[:, cols])
    sub = s_ref[:, :rows]
    eye = lax.broadcasted_iota(jnp.int32, sub.shape, 0) == lax.broadcasted_iota(jnp.int32, sub.shape, 1)
    diag_ref[...] = jnp.sum(jnp.where(eye, sub, 0.0), axis=0, keepdims=True)
    row_ref[...] = rows_of(s_ref, None)
    for store in stores:
        store.wait()


def x_logits_kernel(order, scale, x_in, t_in, s_out, row_ref, col_ref, x, t, s_ref, sems, out_sems):
    rows = x.shape[0]
    copies = fetch([x_in] + [quarter(order, t_in, k, rows) for k in range(4)], [x] + [t.at[k] for k in range(4)], sems)
    mult = scale[0] * LOG2E
    copies[0].wait()
    stores = []
    for k in range(4):
        copies[1 + k].wait()
        cols = slice(k * rows, (k + 1) * rows)
        s_ref[:, cols] = mult * lax.dot_general(x[...], t[k], NT, preferred_element_type=F32)
        stores.append(pltpu.make_async_copy(s_ref.at[:, cols], s_out.at[:, cols], out_sems.at[k]))
        stores[-1].start()
        col_ref[:, cols] = columns_of(s_ref[:, cols])
    row_ref[...] = rows_of(s_ref, None)
    for store in stores:
        store.wait()


def first_logits_kernel(even, scale, a_in, y_in, x_in, v_in, s_ref, row_ref, col_ref, yx_ref, v, sems):
    rows = a_in.shape[0]
    y_copy = fetch_y(even, a_in, y_in, yx_ref.at[:rows, :], sems.at[3])
    copies = fetch([x_in] + halves(v_in, rows), [yx_ref.at[rows:, :], v.at[0], v.at[1]], sems)
    mult = scale[0] * LOG2E
    y_copy.wait()
    copies[0].wait()
    for k in range(2):
        copies[1 + k].wait()
        cols = slice(k * rows, (k + 1) * rows)
        s_ref[:, cols] = mult * lax.dot_general(yx_ref[...], v[k], NT, preferred_element_type=F32)
        col_ref[:, cols] = columns_of(s_ref[:, cols])
    row_ref[...] = rows_of(s_ref, None)


def far_logits_kernel(scale, before, yx, v_in, s_ref, row_ref, col_ref, v, sems):
    rows = v.shape[1]
    copies = fetch(halves(v_in, rows), [v.at[k] for k in range(2)], sems)
    mult = scale[0] * LOG2E
    for k in range(2):
        copies[k].wait()
        cols = slice(k * rows, (k + 1) * rows)
        s_ref[:, cols] = mult * lax.dot_general(yx[...], v[k], NT, preferred_element_type=F32)
        col_ref[:, cols] = columns_of(s_ref[:, cols])
    row_ref[...] = rows_of(s_ref, spread(before[...]))


def weights_of(s_ref, r, c_ref, k, rows, diagonal=False):
    parts = []
    for o in range(k * rows, (k + 1) * rows, LANES):
        z = s_ref[:, o:o + LANES]
        avg = 0.5 * (jnp.exp2(z - r) + jnp.exp2(z - c_ref[:, o:o + LANES]))
        if diagonal:
            ri = lax.broadcasted_iota(jnp.int32, avg.shape, 0)
            ci = lax.broadcasted_iota(jnp.int32, avg.shape, 1) + o
            avg = avg - jnp.where(ri == ci, 1.0, 0.0)
        parts.append(avg.astype(BF16))
    return jnp.concatenate(parts, 1)


def far_text_kernel(scale, row, col, s, yx, w_ref, g_ref):
    rows = yx.shape[0] // 2
    r = spread(row[...])
    for k in (1, 0):
        w = weights_of(s, r, col, k, rows)
        w_ref[:, k * rows:(k + 1) * rows] = w
        g = lax.dot_general(w, yx[...], TN, preferred_element_type=F32)
        g_ref[k * rows:(k + 1) * rows, :] = (scale[0] * g).astype(g_ref.dtype)


def own_text_kernel(scale, row, col, si_in, sx_in, a_in, yx, w_ref, send_ref, keep_ref, s, a, sems):
    rows = a.shape[0]
    sources, targets = [a_in], [a]
    for k in (2, 3, 0, 1):
        cols = slice(k * rows, (k + 1) * rows)
        sources += [si_in.at[:, cols], sx_in.at[:, cols]]
        targets += [s.at[:rows, cols], s.at[rows:, cols]]
    copies = fetch(sources, targets, sems)
    r = spread(row[...])
    for i, k in enumerate((2, 3, 0, 1)):
        copies[1 + 2 * i].wait()
        copies[2 + 2 * i].wait()
        w = weights_of(s, r, col, k, rows, k == 0)
        w_ref[:, k * rows:(k + 1) * rows] = w
        if i == 0:
            copies[0].wait()
        g = lax.dot_general(w[:rows], a[...], TN, preferred_element_type=F32)
        g = scale[0] * (g + lax.dot_general(w[rows:], yx[rows:, :], TN, preferred_element_type=F32))
        if k >= 2:
            send_ref[(k - 2) * rows:(k - 1) * rows, :] = g.astype(send_ref.dtype)
        else:
            keep_ref[k * rows:(k + 1) * rows, :] = g


def y_grads_kernel(scale, wa, wb, va, vb, g_ref, send_ref, v, sems):
    rows = v.shape[1]
    copies = fetch(halves(va, rows) + halves(vb, rows), [v.at[k] for k in range(4)], sems)
    step = 512
    for o in range(0, g_ref.shape[1], step):
        cols = slice(o, o + step)
        g = 0.0
        for k in range(4):
            if o == 0:
                copies[k].wait()
            w = (wa, wb)[k // 2][:rows, (k % 2) * rows:(k % 2 + 1) * rows]
            g = g + jnp.dot(w, v[k, :, cols], preferred_element_type=F32)
        g_ref[:, cols] = scale[0] * g
        send_ref[:, cols] = (scale[0] * g).astype(BF16)


def image_kernel(order, even, scale, w, t_in, wa, wb, va, vb, gy, gi_ref, gx_ref, t, v, sems):
    rows = t.shape[1]
    sources = [quarter(order, t_in, k, rows) for k in range(4)] + halves(va, rows) + halves(vb, rows)
    copies = fetch(sources, [t.at[k] for k in range(4)] + [v.at[k] for k in range(4)], sems)
    step = 512
    for o in range(0, gi_ref.shape[1], step):
        cols = slice(o, o + step)
        gi = gx = 0.0
        for k in range(4):
            if o == 0:
                copies[k].wait()
                copies[4 + k].wait()
            tk = t[k, :, cols]
            wk = w[:, k * rows:(k + 1) * rows]
            gx = gx + jnp.dot(wk[rows:], tk, preferred_element_type=F32)
            gi = gi + jnp.dot(wk[:rows], tk, preferred_element_type=F32)
            far = (wa, wb)[k // 2][rows:, (k % 2) * rows:(k % 2 + 1) * rows]
            gx = gx + jnp.dot(far, v[k, :, cols], preferred_element_type=F32)
        gi_ref[:, cols] = scale[0] * gi + jnp.where(even[0] == 1, 0.0, gy[:, cols])
        gx_ref[:, cols] = (scale[0] * gx).astype(BF16)


def lse2(*parts):
    top = parts[0]
    for p in parts[1:]:
        top = jnp.maximum(top, p)
    total = sum(jnp.exp2(p - top) for p in parts)
    return top + jnp.log2(total)


def tie(*values):
    return lax.optimization_barrier(values)


def per_device(image_emb, text_emb, logit_scale):
    rows, d = image_emb.shape
    blocks = lax.axis_size("blk")
    rep = lax.axis_index("rep")
    even = lax.axis_index("blk") % 2 == 0
    evens = even.astype(jnp.int32).reshape(1)
    order = jnp.stack([rep ^ m for m in ORDER]).astype(jnp.int32)
    x_route = [(i, (i - 1) % blocks if i % 2 == 0 else (i - 3) % blocks) for i in range(blocks)]
    y_route = [(i, (i - 4) % blocks) for i in range(0, blocks, 2)]
    v_route = [(i, i ^ 1) for i in range(blocks)]
    x_back = [(b, a) for a, b in x_route]
    y_back = [(b, a) for a, b in y_route]
    tile = 2 * rows * rows * d

    def hop(value, route):
        return lax.ppermute(value, "blk", route)

    def swap(value, mask):
        return lax.ppermute(value, "rep", [(i, i ^ mask) for i in range(4)])

    def sems(n):
        return pltpu.SemaphoreType.DMA((n,))

    image_buf = pltpu.VMEM((rows, d), BF16)

    half = pl.pallas_call(
        slice_kernel,
        grid_spec=pltpu.PrefetchScalarGridSpec(
            num_scalar_prefetch=1, grid=(2,),
            in_specs=[pl.BlockSpec((rows, d), lambda k, o: (o[k], 0))],
            out_specs=pl.BlockSpec((rows, d), lambda k, o: (k, 0))),
        out_shape=jax.ShapeDtypeStruct((2 * rows, d), BF16),
        name="quarters",
    )(order, text_emb)
    half, images = tie(half, image_emb)
    va = hop(half, v_route)
    x = hop(images, x_route)
    y = hop(images, y_route)
    wide, narrow = (1, 4 * rows), (1, rows)
    text_buf = pltpu.VMEM((4, rows, d), BF16)
    half_buf = pltpu.VMEM((2, rows, d), BF16)
    logits_buf = pltpu.VMEM((rows, 4 * rows), F32)

    logits_i, r_i, col_i, diag = local_call(
        own_image_kernel, "own_image", [SMEM] * 2 + [HBM] * 2,
        [((rows, 4 * rows), F32), (narrow, F32), (wide, F32), (narrow, F32)], 4 * tile,
        [image_buf, text_buf, logits_buf, sems(5), sems(4)], [HBM, VMEM, VMEM, VMEM],
    )(order, logit_scale, image_emb, text_emb)
    x, logits_i = tie(x, logits_i)
    logits_x, r_xt, col_x = local_call(
        x_logits_kernel, "x_logits", [SMEM] * 2 + [HBM] * 2,
        [((rows, 4 * rows), F32), (narrow, F32), (wide, F32)], 4 * tile,
        [image_buf, text_buf, logits_buf, sems(5), sems(4)], [HBM, VMEM, VMEM],
    )(order, logit_scale, x, text_emb)
    h_y = hop(r_i, y_route)
    va, y, r_xt, logits_x, h_y = tie(va, y, r_xt, logits_x, h_y)
    vb = swap(va, 1)
    s_a, row_a, col_a, yx = local_call(
        first_logits_kernel, "first_logits", [SMEM] * 2 + [HBM] * 4,
        [((2 * rows, 2 * rows), F32), ((1, 2 * rows), F32), ((1, 2 * rows), F32), ((2 * rows, d), BF16)], 4 * tile,
        [half_buf, sems(4)],
    )(evens, logit_scale, image_emb, y, x, va)
    s_b, row_v, col_b = local_call(
        far_logits_kernel, "far_logits", [SMEM, VMEM, VMEM, HBM],
        [((2 * rows, 2 * rows), F32), ((1, 2 * rows), F32), ((1, 2 * rows), F32)], 4 * tile,
        [half_buf, sems(2)],
    )(logit_scale, row_a, yx, vb)

    r_y, r_xv = row_v[:, :rows], row_v[:, rows:]
    r_x = lse2(r_xt, r_xv)
    h_i = jnp.where(even, r_i, lse2(r_i, r_y))
    col_t = lse2(col_i, col_x)
    col_v = jnp.concatenate([col_a, col_b], 1)
    blank = jnp.zeros((1, 3 * rows), F32)
    peer = hop(jnp.concatenate([col_v, col_t, jnp.concatenate([diag, blank], 1)]), v_route)
    down = hop(jnp.concatenate([h_i, r_x], 1), x_route)
    up = hop(jnp.concatenate([r_x, r_y], 1), x_back)
    y_i = hop(r_y, y_back)
    peer, down, up, y_i = tie(peer, down, up, y_i)
    h_x, x_y = down[:, :rows], down[:, rows:]
    x_i, y_x = up[:, :rows], up[:, rows:]
    row_x = jnp.where(even, lse2(h_x, r_x), lse2(h_x, r_x, y_x))
    row_i = jnp.where(even, lse2(r_i, x_i, y_i), lse2(h_i, x_i))
    row_y = jnp.where(even, lse2(r_y, h_y, x_y), row_i)
    row_yx = jnp.concatenate([row_y, row_x], 1)
    row_ix = jnp.concatenate([row_i, row_x], 1)
    pair = row_i + row_x - 2.0 * (diag + peer[2:, :rows])
    columns = jnp.concatenate([lse2(col_t, peer[:1]), lse2(col_v, peer[1:2])])
    stats = jnp.concatenate([columns, jnp.concatenate([pair, blank], 1)])
    got = [swap(stats, mask) for mask in (1, 2, 3)]
    aligned = [columns]
    for mask, g in zip((1, 2, 3), got):
        places = [PLACE[ORDER[k] ^ mask] for k in range(4)]
        aligned.append(jnp.concatenate([g[:2, p * rows:(p + 1) * rows] for p in places], 1))
    columns = lse2(*aligned)
    c_t, c_v = columns[:1], columns[1:]
    pair = sum((g[2:, :rows] for g in got), pair)
    column_sum = c_t + c_v
    loss_part = LN2 * sum((column_sum[:, k * rows:(k + 1) * rows] for k in range(4)), pair)

    def far_text(s, cols, dtype):
        return local_call(
            far_text_kernel, "far_text", [SMEM] + [VMEM] * 4,
            [((2 * rows, 2 * rows), BF16), ((2 * rows, d), dtype)], 4 * tile,
        )(logit_scale, row_yx, cols, s, yx)

    def cross(value, mask):
        return hop(value, [(i, i ^ mask) for i in range(blocks)])

    def ring(value, distance):
        span = blocks // 2
        return hop(value, [((i + 4 * distance) % span + i // span * span, i) for i in range(blocks)])

    w_b, send_v = far_text(s_b, c_v[:, 2 * rows:], CORE_V)
    send_v, s_a = tie(send_v, s_a)
    got_v = swap(send_v, 1)
    got = cross(loss_part, 2)
    w_a, keep_v = far_text(s_a, c_v[:, :2 * rows], F32)
    keep_v, got_v, got = tie(keep_v, got_v, got)
    loss_part = loss_part + got
    v_one = (keep_v[rows:] + got_v[rows:].astype(F32)).astype(BF16)
    v_zero = (keep_v[:rows] + got_v[:rows].astype(F32)).astype(BF16)
    v_one, v_zero, logits_x, loss_part, w_a = tie(v_one, v_zero, logits_x, loss_part, w_a)
    home_1 = hop(v_one, v_route)
    home_0 = hop(v_zero, v_route)
    g_y, g_y_send = local_call(
        y_grads_kernel, "y_grads", [SMEM] + [VMEM] * 2 + [HBM] * 2,
        [((rows, d), F32), ((rows, d), BF16)], 4 * tile, [text_buf, sems(4)],
    )(logit_scale, w_a, w_b, va, vb)
    y_got = hop(g_y_send, y_back)
    logits_x, g_y, loss_part = tie(logits_x, g_y, loss_part)
    got = cross(loss_part, blocks // 2)
    w_t, send_t, keep_t = local_call(
        own_text_kernel, "own_text", [SMEM] + [VMEM] * 2 + [HBM] * 3 + [VMEM],
        [((2 * rows, 4 * rows), BF16), ((2 * rows, d), CORE), ((2 * rows, d), F32)], 8 * tile,
        [pltpu.VMEM((2 * rows, 4 * rows), F32), image_buf, sems(9)],
    )(logit_scale, row_ix, c_t, logits_i, logits_x, image_emb, yx)
    send_t, got = tie(send_t, got)
    loss_part = loss_part + got
    got_one = swap(send_t[rows:], 1)
    got_zero = swap(send_t[:rows], 1)
    got = ring(loss_part, 1)
    g_i, g_x = local_call(
        image_kernel, "image_grads", [SMEM] * 3 + [VMEM, HBM, VMEM, VMEM, HBM, HBM, VMEM],
        [((rows, d), F32), ((rows, d), BF16)], 16 * tile, [text_buf, text_buf, sems(8)],
    )(order, evens, logit_scale, w_t, text_emb, w_a, w_b, va, vb, g_y)
    g_x, got, got_one = tie(g_x, got, got_one)
    loss_part = loss_part + got
    x_got = hop(g_x, x_back)
    loss_part = loss_part + ring(loss_part, 2)
    part = keep_t[rows:] + got_one.astype(F32)
    part, home_1, loss_part = tie(part, home_1, loss_part)
    one = (part + home_1.astype(F32)).astype(BF16)
    one, loss_part = tie(one, loss_part)
    across = swap(one, 2)
    loss_part = loss_part + ring(loss_part, 4)
    loss = jnp.sum(loss_part, axis=1) / (2.0 * rows * blocks * 4)
    base = keep_t[:rows] + got_zero.astype(F32)
    grad_text = base + home_0.astype(F32) + across.astype(F32)
    grad_image = g_i + x_got.astype(F32) + jnp.where(even, y_got, jnp.zeros_like(y_got)).astype(F32)
    return grad_image, grad_text, loss


def solution(mesh):
    placed = (P(("blk", "rep"), None), P("blk", None), P())
    return jax.shard_map(
        per_device,
        mesh=mesh,
        in_specs=placed,
        out_specs=(P(("blk", "rep"), None), P(("blk", "rep"), None), P()),
        check_vma=False,
    )
```

```python
import math

import jax
import jax.numpy as jnp
from jax import lax
from jax.experimental import pallas as pl
from jax.experimental.pallas import tpu as pltpu
from jax.sharding import PartitionSpec as P

LOG2E = math.log2(math.e)
LN2 = math.log(2.0)
ORDER = (0, 2, 1, 3)
PLACE = (0, 2, 1, 3)
NT = (((1,), (1,)), ((), ()))
TN = (((0,), (0,)), ((), ()))
F32 = jnp.float32
BF16 = jnp.bfloat16
CORE = jnp.bfloat16
CORE_V = jnp.float32
LANES = 128
VMEM = pl.BlockSpec(memory_space=pltpu.VMEM)
SMEM = pl.BlockSpec(memory_space=pltpu.SMEM)


ANY = pl.BlockSpec(memory_space=pl.ANY)
HBM = pl.BlockSpec(memory_space=pltpu.HBM)


def local_call(kernel, name, specs, shapes, flops, scratch=(), out_specs=None):
    return pl.pallas_call(
        kernel,
        in_specs=specs,
        out_specs=out_specs or [VMEM] * len(shapes),
        out_shape=[jax.ShapeDtypeStruct(*s) for s in shapes],
        scratch_shapes=list(scratch),
        compiler_params=pltpu.CompilerParams(vmem_limit_bytes=16 * 1024 * 1024),
        cost_estimate=pl.CostEstimate(flops=1, bytes_accessed=1, transcendentals=0),
        name=name,
    )


def fetch(sources, targets, sems):
    copies = [pltpu.make_async_copy(s, t, sems.at[i]) for i, (s, t) in enumerate(zip(sources, targets))]
    for copy in copies:
        copy.start()
    return copies


def fetch_y(even, a, y, target, sem):
    @pl.when(even[0] == 1)
    def _():
        pltpu.make_async_copy(y, target, sem).start()

    @pl.when(even[0] != 1)
    def _():
        pltpu.make_async_copy(a, target, sem).start()

    return pltpu.make_async_copy(y, target, sem)


def columns_of(s):
    top = jnp.max(s, axis=0, keepdims=True)
    return top + jnp.log2(jnp.sum(jnp.exp2(s - top), axis=0, keepdims=True))


def rows_of(s_ref, before):
    slabs = range(0, s_ref.shape[1], LANES)
    m = s_ref[:, :LANES]
    for o in slabs[1:]:
        m = jnp.maximum(m, s_ref[:, o:o + LANES])
    top = jnp.max(m, axis=1, keepdims=True)
    if before is not None:
        top = jnp.maximum(top, before)
    else:
        top = jnp.broadcast_to(top, m.shape)
    part = jnp.exp2(s_ref[:, :LANES] - top)
    for o in slabs[1:]:
        part = part + jnp.exp2(s_ref[:, o:o + LANES] - top)
    total = jnp.sum(part, axis=1, keepdims=True)
    if before is not None:
        total = total + jnp.exp2(before - top)
    return jnp.transpose(top + jnp.log2(total))[:1, :]


def spread(vec):
    return jnp.transpose(jnp.broadcast_to(vec, (LANES, vec.shape[1])))


def quarter(order, t, k, rows):
    return t.at[pl.ds(pl.multiple_of(order[k] * rows, rows), rows), :]


def halves(ref, rows):
    return [ref.at[k * rows:(k + 1) * rows, :] for k in range(2)]


def own_image_kernel(order, scale, a_in, t_in, s_out, row_ref, col_ref, diag_ref, a, t, s_ref, sems, out_sems):
    rows = a.shape[0]
    copies = fetch([a_in] + [quarter(order, t_in, k, rows) for k in range(4)], [a] + [t.at[k] for k in range(4)], sems)
    mult = scale[0] * LOG2E
    copies[0].wait()
    stores = []
    for k in range(4):
        copies[1 + k].wait()
        cols = slice(k * rows, (k + 1) * rows)
        s_ref[:, cols] = mult * lax.dot_general(a[...], t[k], NT, preferred_element_type=F32)
        stores.append(pltpu.make_async_copy(s_ref.at[:, cols], s_out.at[:, cols], out_sems.at[k]))
        stores[-1].start()
        col_ref[:, cols] = columns_of(s_ref[:, cols])
    sub = s_ref[:, :rows]
    eye = lax.broadcasted_iota(jnp.int32, sub.shape, 0) == lax.broadcasted_iota(jnp.int32, sub.shape, 1)
    diag_ref[...] = jnp.sum(jnp.where(eye, sub, 0.0), axis=0, keepdims=True)
    row_ref[...] = rows_of(s_ref, None)
    for store in stores:
        store.wait()


def x_logits_kernel(order, scale, x_in, t_in, s_out, row_ref, col_ref, x, t, s_ref, sems, out_sems):
    rows = x.shape[0]
    copies = fetch([x_in] + [quarter(order, t_in, k, rows) for k in range(4)], [x] + [t.at[k] for k in range(4)], sems)
    mult = scale[0] * LOG2E
    copies[0].wait()
    stores = []
    for k in range(4):
        copies[1 + k].wait()
        cols = slice(k * rows, (k + 1) * rows)
        s_ref[:, cols] = mult * lax.dot_general(x[...], t[k], NT, preferred_element_type=F32)
        stores.append(pltpu.make_async_copy(s_ref.at[:, cols], s_out.at[:, cols], out_sems.at[k]))
        stores[-1].start()
        col_ref[:, cols] = columns_of(s_ref[:, cols])
    row_ref[...] = rows_of(s_ref, None)
    for store in stores:
        store.wait()


def first_logits_kernel(even, scale, a_in, y_in, x_in, v_in, s_ref, row_ref, col_ref, yx_ref, v, sems):
    rows = a_in.shape[0]
    y_copy = fetch_y(even, a_in, y_in, yx_ref.at[:rows, :], sems.at[3])
    copies = fetch([x_in] + halves(v_in, rows), [yx_ref.at[rows:, :]] + halves(v, rows), sems)
    mult = scale[0] * LOG2E
    y_copy.wait()
    copies[0].wait()
    for k in range(2):
        copies[1 + k].wait()
        cols = slice(k * rows, (k + 1) * rows)
        s_ref[:, cols] = mult * lax.dot_general(yx_ref[...], v[cols, :], NT, preferred_element_type=F32)
        col_ref[:, cols] = columns_of(s_ref[:, cols])
    row_ref[...] = rows_of(s_ref, None)


def far_logits_kernel(scale, before, yx, v_in, s_ref, row_ref, col_ref, v, sems):
    rows = v.shape[0] // 2
    copies = fetch(halves(v_in, rows), halves(v, rows), sems)
    mult = scale[0] * LOG2E
    for k in range(2):
        copies[k].wait()
        cols = slice(k * rows, (k + 1) * rows)
        s_ref[:, cols] = mult * lax.dot_general(yx[...], v[cols, :], NT, preferred_element_type=F32)
        col_ref[:, cols] = columns_of(s_ref[:, cols])
    row_ref[...] = rows_of(s_ref, spread(before[...]))


def weights_of(s_ref, r, c_ref, k, rows, diagonal=False):
    parts = []
    for o in range(k * rows, (k + 1) * rows, LANES):
        z = s_ref[:, o:o + LANES]
        avg = 0.5 * (jnp.exp2(z - r) + jnp.exp2(z - c_ref[:, o:o + LANES]))
        if diagonal:
            ri = lax.broadcasted_iota(jnp.int32, avg.shape, 0)
            ci = lax.broadcasted_iota(jnp.int32, avg.shape, 1) + o
            avg = avg - jnp.where(ri == ci, 1.0, 0.0)
        parts.append(avg.astype(BF16))
    return jnp.concatenate(parts, 1)


def far_text_kernel(scale, row, col, s, yx, w_ref, g_ref):
    rows = yx.shape[0] // 2
    r = spread(row[...])
    for k in (1, 0):
        w = weights_of(s, r, col, k, rows)
        w_ref[:, k * rows:(k + 1) * rows] = w
        g = lax.dot_general(w, yx[...], TN, preferred_element_type=F32)
        g_ref[k * rows:(k + 1) * rows, :] = (scale[0] * g).astype(g_ref.dtype)


def own_text_kernel(scale, row, col, si_in, sx_in, a_in, yx, w_ref, send_ref, keep_ref, s, a, sems):
    rows = a.shape[0]
    sources, targets = [a_in], [a]
    for k in (2, 3, 0, 1):
        cols = slice(k * rows, (k + 1) * rows)
        sources += [si_in.at[:, cols], sx_in.at[:, cols]]
        targets += [s.at[:rows, cols], s.at[rows:, cols]]
    copies = fetch(sources, targets, sems)
    r = spread(row[...])
    for i, k in enumerate((2, 3, 0, 1)):
        copies[1 + 2 * i].wait()
        copies[2 + 2 * i].wait()
        w = weights_of(s, r, col, k, rows, k == 0)
        w_ref[:, k * rows:(k + 1) * rows] = w
        if i == 0:
            copies[0].wait()
        g = lax.dot_general(w[:rows], a[...], TN, preferred_element_type=F32)
        g = scale[0] * (g + lax.dot_general(w[rows:], yx[rows:, :], TN, preferred_element_type=F32))
        if k >= 2:
            send_ref[(k - 2) * rows:(k - 1) * rows, :] = g.astype(send_ref.dtype)
        else:
            keep_ref[k * rows:(k + 1) * rows, :] = g


def y_grads_kernel(scale, wa, wb, va, vb, g_ref, send_ref):
    rows = wa.shape[0] // 2
    g = jnp.dot(wa[:rows, :], va[...], preferred_element_type=F32)
    g = scale[0] * (g + jnp.dot(wb[:rows, :], vb[...], preferred_element_type=F32))
    g_ref[...] = g
    send_ref[...] = g.astype(BF16)


def image_kernel(order, even, scale, w, t_in, wa, wb, va, vb, gy, gi_ref, gx_ref, t, sems):
    rows = t.shape[1]
    copies = fetch([quarter(order, t_in, k, rows) for k in range(4)], [t.at[k] for k in range(4)], sems)
    step = 512
    for o in range(0, gi_ref.shape[1], step):
        cols = slice(o, o + step)
        gx = jnp.dot(wa[rows:, :], va[:, cols], preferred_element_type=F32)
        gx = gx + jnp.dot(wb[rows:, :], vb[:, cols], preferred_element_type=F32)
        gi = 0.0
        for k in range(4):
            if o == 0:
                copies[k].wait()
            tk = t[k, :, cols]
            wk = w[:, k * rows:(k + 1) * rows]
            gx = gx + jnp.dot(wk[rows:], tk, preferred_element_type=F32)
            gi = gi + jnp.dot(wk[:rows], tk, preferred_element_type=F32)
        gi_ref[:, cols] = scale[0] * gi + jnp.where(even[0] == 1, 0.0, gy[:, cols])
        gx_ref[:, cols] = (scale[0] * gx).astype(BF16)


def finish_kernel(keep, got_zero, home_0, across, g_i, x_got, y_got, loss_in, scale_in, text_out, image_out, loss_ref,
                  b0, b1, b2, b3, b4, out, sems, out_sems):
    rows, d = b0.shape
    span = d // 2
    parts = [slice(0, span), slice(span, d)]
    texts = [fetch([r.at[:, c] for r in (got_zero, home_0, across)], [b.at[:, c] for b in (b0, b1, b2)], sems.at[i])
             for i, c in enumerate(parts)]
    images = [fetch([r.at[:, c] for r in (x_got, y_got)], [b.at[:, c] for b in (b3, b4)], sems.at[2 + i])
              for i, c in enumerate(parts)]
    loss_ref[...] = jnp.sum(loss_in[...], axis=1, keepdims=True) * scale_in[0]
    stores = []
    for i, c in enumerate(parts):
        for copy in images[i]:
            copy.wait()
        out[0, :, c] = g_i[:, c] + b3[:, c].astype(F32) + b4[:, c].astype(F32)
        stores.append(pltpu.make_async_copy(out.at[0, :, c], image_out.at[:, c], out_sems.at[2 * i]))
        stores[-1].start()
        for copy in texts[i]:
            copy.wait()
        total = keep[:rows, c] + b0[:, c].astype(F32) + b1[:, c].astype(F32) + b2[:, c].astype(F32)
        out[1, :, c] = total
        stores.append(pltpu.make_async_copy(out.at[1, :, c], text_out.at[:, c], out_sems.at[2 * i + 1]))
        stores[-1].start()
    for store in stores:
        store.wait()


def lse2(*parts):
    top = parts[0]
    for p in parts[1:]:
        top = jnp.maximum(top, p)
    total = sum(jnp.exp2(p - top) for p in parts)
    return top + jnp.log2(total)


def tie(*values):
    return lax.optimization_barrier(values)


def per_device(image_emb, text_emb, logit_scale):
    rows, d = image_emb.shape
    blocks = lax.axis_size("blk")
    rep = lax.axis_index("rep")
    even = lax.axis_index("blk") % 2 == 0
    evens = even.astype(jnp.int32).reshape(1)
    order = jnp.stack([rep ^ m for m in ORDER]).astype(jnp.int32)
    x_route = [(i, (i - 1) % blocks if i % 2 == 0 else (i - 3) % blocks) for i in range(blocks)]
    y_route = [(i, (i - 4) % blocks) for i in range(0, blocks, 2)]
    v_route = [(i, i ^ 1) for i in range(blocks)]
    x_back = [(b, a) for a, b in x_route]
    y_back = [(b, a) for a, b in y_route]
    tile = 2 * rows * rows * d

    def hop(value, route):
        return lax.ppermute(value, "blk", route)

    def swap(value, mask):
        return lax.ppermute(value, "rep", [(i, i ^ mask) for i in range(4)])

    def sems(n):
        return pltpu.SemaphoreType.DMA((n,))

    image_buf = pltpu.VMEM((rows, d), BF16)

    half = jnp.concatenate([lax.dynamic_slice_in_dim(text_emb, (rep ^ m) * rows, rows, 0) for m in ORDER[:2]])
    half, images = tie(half, image_emb)
    va = hop(half, v_route)
    x = hop(images, x_route)
    y = hop(images, y_route)
    wide, narrow = (1, 4 * rows), (1, rows)
    text_buf = pltpu.VMEM((4, rows, d), BF16)
    logits_buf = pltpu.VMEM((rows, 4 * rows), F32)

    logits_i, r_i, col_i, diag = local_call(
        own_image_kernel, "own_image", [SMEM] * 2 + [HBM] * 2,
        [((rows, 4 * rows), F32), (narrow, F32), (wide, F32), (narrow, F32)], 4 * tile,
        [image_buf, text_buf, logits_buf, sems(5), sems(4)], [HBM, VMEM, VMEM, VMEM],
    )(order, logit_scale, image_emb, text_emb)
    x, logits_i = tie(x, logits_i)
    logits_x, r_xt, col_x = local_call(
        x_logits_kernel, "x_logits", [SMEM] * 2 + [HBM] * 2,
        [((rows, 4 * rows), F32), (narrow, F32), (wide, F32)], 4 * tile,
        [image_buf, text_buf, logits_buf, sems(5), sems(4)], [HBM, VMEM, VMEM],
    )(order, logit_scale, x, text_emb)
    h_y = hop(r_i, y_route)
    va, y, r_xt, logits_x, h_y = tie(va, y, r_xt, logits_x, h_y)
    vb = swap(va, 1)
    s_a, row_a, col_a, yx, near_a = local_call(
        first_logits_kernel, "first_logits", [SMEM] * 2 + [HBM] * 4,
        [((2 * rows, 2 * rows), F32), ((1, 2 * rows), F32), ((1, 2 * rows), F32)] + [((2 * rows, d), BF16)] * 2, 4 * tile,
        [sems(4)],
    )(evens, logit_scale, image_emb, y, x, va)
    s_b, row_v, col_b, near_b = local_call(
        far_logits_kernel, "far_logits", [SMEM, VMEM, VMEM, HBM],
        [((2 * rows, 2 * rows), F32), ((1, 2 * rows), F32), ((1, 2 * rows), F32), ((2 * rows, d), BF16)], 4 * tile,
        [sems(2)],
    )(logit_scale, row_a, yx, vb)

    r_y, r_xv = row_v[:, :rows], row_v[:, rows:]
    r_x = lse2(r_xt, r_xv)
    h_i = jnp.where(even, r_i, lse2(r_i, r_y))
    col_t = lse2(col_i, col_x)
    col_v = jnp.concatenate([col_a, col_b], 1)
    blank = jnp.zeros((1, 3 * rows), F32)
    peer = hop(jnp.concatenate([col_v, col_t, jnp.concatenate([diag, blank], 1)]), v_route)
    down = hop(jnp.concatenate([h_i, r_x], 1), x_route)
    up = hop(jnp.concatenate([r_x, r_y], 1), x_back)
    y_i = hop(r_y, y_back)
    peer, down, up, y_i = tie(peer, down, up, y_i)
    h_x, x_y = down[:, :rows], down[:, rows:]
    x_i, y_x = up[:, :rows], up[:, rows:]
    row_x = jnp.where(even, lse2(h_x, r_x), lse2(h_x, r_x, y_x))
    row_i = jnp.where(even, lse2(r_i, x_i, y_i), lse2(h_i, x_i))
    row_y = jnp.where(even, lse2(r_y, h_y, x_y), row_i)
    row_yx = jnp.concatenate([row_y, row_x], 1)
    row_ix = jnp.concatenate([row_i, row_x], 1)
    pair = row_i + row_x - 2.0 * (diag + peer[2:, :rows])
    columns = jnp.concatenate([lse2(col_t, peer[:1]), lse2(col_v, peer[1:2])])
    stats = jnp.concatenate([columns, jnp.concatenate([pair, blank], 1)])
    got = [swap(stats, mask) for mask in (1, 2, 3)]
    aligned = [columns]
    for mask, g in zip((1, 2, 3), got):
        places = [PLACE[ORDER[k] ^ mask] for k in range(4)]
        aligned.append(jnp.concatenate([g[:2, p * rows:(p + 1) * rows] for p in places], 1))
    columns = lse2(*aligned)
    c_t, c_v = columns[:1], columns[1:]
    pair = sum((g[2:, :rows] for g in got), pair)
    column_sum = c_t + c_v
    loss_part = LN2 * sum((column_sum[:, k * rows:(k + 1) * rows] for k in range(4)), pair)

    def far_text(s, cols, dtype):
        return local_call(
            far_text_kernel, "far_text", [SMEM] + [VMEM] * 4,
            [((2 * rows, 2 * rows), BF16), ((2 * rows, d), dtype)], 4 * tile,
        )(logit_scale, row_yx, cols, s, yx)

    def shifted(value, xor, distance):
        span = blocks // 2

        def source(i):
            i = i ^ xor
            return (i + 4 * distance) % span + i // span * span
        return hop(value, [(source(i), i) for i in range(blocks)])

    w_t, send_t, keep_t = local_call(
        own_text_kernel, "own_text", [SMEM] + [VMEM] * 2 + [HBM] * 3 + [VMEM],
        [((2 * rows, 4 * rows), BF16), ((2 * rows, d), CORE), ((2 * rows, d), F32)], 8 * tile,
        [pltpu.VMEM((2 * rows, 4 * rows), F32), image_buf, sems(9)],
    )(logit_scale, row_ix, c_t, logits_i, logits_x, image_emb, yx)
    got_t = swap(send_t, 1)
    send_t, s_b = tie(send_t, s_b)
    w_b, send_v = far_text(s_b, c_v[:, 2 * rows:], CORE_V)
    send_v, s_a = tie(send_v, s_a)
    got_v = swap(send_v, 1)
    got = shifted(loss_part, 2, 0)
    w_a, keep_v = far_text(s_a, c_v[:, :2 * rows], F32)
    keep_v, got_v, got, got_t = tie(keep_v, got_v, got, got_t)
    loss_part = loss_part + got
    v_one = (keep_v[rows:] + got_v[rows:].astype(F32)).astype(BF16)
    v_zero = (keep_v[:rows] + got_v[:rows].astype(F32)).astype(BF16)
    v_one, v_zero, loss_part, w_a = tie(v_one, v_zero, loss_part, w_a)
    home_1 = hop(v_one, v_route)
    home_0 = hop(v_zero, v_route)
    g_y, g_y_send = local_call(
        y_grads_kernel, "y_grads", [SMEM] + [VMEM] * 4, [((rows, d), F32), ((rows, d), BF16)], 4 * tile,
    )(logit_scale, w_a, w_b, near_a, near_b)
    y_got = hop(g_y_send, y_back)
    g_i, g_x = local_call(
        image_kernel, "image_grads", [SMEM] * 3 + [VMEM, HBM] + [VMEM] * 5,
        [((rows, d), F32), ((rows, d), BF16)], 16 * tile, [text_buf, sems(4)],
    )(order, evens, logit_scale, w_t, text_emb, w_a, w_b, near_a, near_b, g_y)
    g_x, loss_part = tie(g_x, loss_part)
    got = [shifted(loss_part, x, z) for x, z in ((blocks // 2, 0), (0, 4), (blocks // 2, 4))]
    got_zero = got_t[:rows]
    part = keep_t[rows:] + got_t[rows:].astype(F32)
    part, home_1, g_i, y_got, *got = tie(part, home_1, g_i, y_got, *got)
    loss_part = sum(got, loss_part)
    one = (part + home_1.astype(F32)).astype(BF16)
    one, loss_part, g_x = tie(one, loss_part, g_x)
    across = swap(one, 2)
    x_got = hop(g_x, x_back)
    got = [shifted(loss_part, 0, z) for z in (1, 2, 3)]
    across, home_0, x_got, *got = tie(across, home_0, x_got, *got)
    grad_text, grad_image, loss = local_call(
        finish_kernel, "finish", [VMEM, ANY, ANY, ANY, VMEM, ANY, ANY, VMEM, SMEM],
        [((rows, d), F32), ((rows, d), F32), ((1, 1), F32)], tile,
        [image_buf] * 5 + [pltpu.VMEM((2, rows, d), F32), pltpu.SemaphoreType.DMA((4, 3)), sems(4)], [ANY, ANY, VMEM],
    )(keep_t, got_zero, home_0, across, g_i, x_got, y_got, sum(got, loss_part),
      jnp.full((1,), 1.0 / (2.0 * rows * blocks * 4), F32))
    return grad_image, grad_text, loss.reshape(1)


def solution(mesh):
    placed = (P(("blk", "rep"), None), P("blk", None), P())
    return jax.shard_map(
        per_device,
        mesh=mesh,
        in_specs=placed,
        out_specs=(P(("blk", "rep"), None), P(("blk", "rep"), None), P()),
        check_vma=False,
    )
```

```python
import math

import jax
import jax.numpy as jnp
from jax import lax
from jax.experimental import pallas as pl
from jax.experimental.pallas import tpu as pltpu
from jax.sharding import PartitionSpec as P

LOG2E = math.log2(math.e)
LN2 = math.log(2.0)
ORDER = (0, 2, 1, 3)
PLACE = (0, 2, 1, 3)
NT = (((1,), (1,)), ((), ()))
TN = (((0,), (0,)), ((), ()))
F32 = jnp.float32
BF16 = jnp.bfloat16
CORE = jnp.bfloat16
CORE_V = jnp.float32
LANES = 128
VMEM = pl.BlockSpec(memory_space=pltpu.VMEM)
SMEM = pl.BlockSpec(memory_space=pltpu.SMEM)


ANY = pl.BlockSpec(memory_space=pl.ANY)
HBM = pl.BlockSpec(memory_space=pltpu.HBM)


def local_call(kernel, name, specs, shapes, flops, scratch=(), out_specs=None):
    return pl.pallas_call(
        kernel,
        in_specs=specs,
        out_specs=out_specs or [VMEM] * len(shapes),
        out_shape=[jax.ShapeDtypeStruct(*s) for s in shapes],
        scratch_shapes=list(scratch),
        compiler_params=pltpu.CompilerParams(vmem_limit_bytes=16 * 1024 * 1024),
        cost_estimate=pl.CostEstimate(flops=1, bytes_accessed=1, transcendentals=0),
        name=name,
    )


def fetch(sources, targets, sems):
    copies = [pltpu.make_async_copy(s, t, sems.at[i]) for i, (s, t) in enumerate(zip(sources, targets))]
    for copy in copies:
        copy.start()
    return copies


def fetch_y(even, a, y, target, sem):
    @pl.when(even[0] == 1)
    def _():
        pltpu.make_async_copy(y, target, sem).start()

    @pl.when(even[0] != 1)
    def _():
        pltpu.make_async_copy(a, target, sem).start()

    return pltpu.make_async_copy(y, target, sem)


def columns_of(s):
    top = jnp.max(s, axis=0, keepdims=True)
    return top + jnp.log2(jnp.sum(jnp.exp2(s - top), axis=0, keepdims=True))


def rows_of(s_ref, before):
    slabs = range(0, s_ref.shape[1], LANES)
    m = s_ref[:, :LANES]
    for o in slabs[1:]:
        m = jnp.maximum(m, s_ref[:, o:o + LANES])
    top = jnp.max(m, axis=1, keepdims=True)
    if before is not None:
        top = jnp.maximum(top, before)
    else:
        top = jnp.broadcast_to(top, m.shape)
    part = jnp.exp2(s_ref[:, :LANES] - top)
    for o in slabs[1:]:
        part = part + jnp.exp2(s_ref[:, o:o + LANES] - top)
    total = jnp.sum(part, axis=1, keepdims=True)
    if before is not None:
        total = total + jnp.exp2(before - top)
    return jnp.transpose(top + jnp.log2(total))[:1, :]


def spread(vec):
    return jnp.transpose(jnp.broadcast_to(vec, (LANES, vec.shape[1])))


def quarter(order, t, k, rows):
    return t.at[pl.ds(pl.multiple_of(order[k] * rows, rows), rows), :]


def halves(ref, rows):
    return [ref.at[k * rows:(k + 1) * rows, :] for k in range(2)]


def own_image_kernel(order, scale, a_in, t_in, s_out, row_ref, col_ref, diag_ref, a, t, s_ref, sems, out_sems):
    rows = a.shape[0]
    copies = fetch([a_in] + [quarter(order, t_in, k, rows) for k in range(4)], [a] + [t.at[k] for k in range(4)], sems)
    mult = scale[0] * LOG2E
    copies[0].wait()
    stores = []
    for k in range(4):
        copies[1 + k].wait()
        cols = slice(k * rows, (k + 1) * rows)
        s_ref[:, cols] = mult * lax.dot_general(a[...], t[k], NT, preferred_element_type=F32)
        stores.append(pltpu.make_async_copy(s_ref.at[:, cols], s_out.at[:, cols], out_sems.at[k]))
        stores[-1].start()
        col_ref[:, cols] = columns_of(s_ref[:, cols])
    sub = s_ref[:, :rows]
    eye = lax.broadcasted_iota(jnp.int32, sub.shape, 0) == lax.broadcasted_iota(jnp.int32, sub.shape, 1)
    diag_ref[...] = jnp.sum(jnp.where(eye, sub, 0.0), axis=0, keepdims=True)
    row_ref[...] = rows_of(s_ref, None)
    for store in stores:
        store.wait()


def x_logits_kernel(order, scale, x_in, t_in, s_out, row_ref, col_ref, x, t, s_ref, sems, out_sems):
    rows = x.shape[0]
    copies = fetch([x_in] + [quarter(order, t_in, k, rows) for k in range(4)], [x] + [t.at[k] for k in range(4)], sems)
    mult = scale[0] * LOG2E
    copies[0].wait()
    stores = []
    for k in range(4):
        copies[1 + k].wait()
        cols = slice(k * rows, (k + 1) * rows)
        s_ref[:, cols] = mult * lax.dot_general(x[...], t[k], NT, preferred_element_type=F32)
        stores.append(pltpu.make_async_copy(s_ref.at[:, cols], s_out.at[:, cols], out_sems.at[k]))
        stores[-1].start()
        col_ref[:, cols] = columns_of(s_ref[:, cols])
    row_ref[...] = rows_of(s_ref, None)
    for store in stores:
        store.wait()


def first_logits_kernel(even, scale, a_in, y_in, x_in, v_in, s_ref, row_ref, col_ref, yx_ref, v, sems):
    rows = a_in.shape[0]
    y_copy = fetch_y(even, a_in, y_in, yx_ref.at[:rows, :], sems.at[3])
    copies = fetch([x_in] + halves(v_in, rows), [yx_ref.at[rows:, :]] + halves(v, rows), sems)
    mult = scale[0] * LOG2E
    y_copy.wait()
    copies[0].wait()
    for k in range(2):
        copies[1 + k].wait()
        cols = slice(k * rows, (k + 1) * rows)
        s_ref[:, cols] = mult * lax.dot_general(yx_ref[...], v[cols, :], NT, preferred_element_type=F32)
        col_ref[:, cols] = columns_of(s_ref[:, cols])
    row_ref[...] = rows_of(s_ref, None)


def far_logits_kernel(scale, before, yx, v_in, s_ref, row_ref, col_ref, v, sems):
    rows = v.shape[0] // 2
    copies = fetch(halves(v_in, rows), halves(v, rows), sems)
    mult = scale[0] * LOG2E
    for k in range(2):
        copies[k].wait()
        cols = slice(k * rows, (k + 1) * rows)
        s_ref[:, cols] = mult * lax.dot_general(yx[...], v[cols, :], NT, preferred_element_type=F32)
        col_ref[:, cols] = columns_of(s_ref[:, cols])
    row_ref[...] = rows_of(s_ref, spread(before[...]))


def weights_of(s_ref, r, c_ref, k, rows, diagonal=False):
    parts = []
    for o in range(k * rows, (k + 1) * rows, LANES):
        z = s_ref[:, o:o + LANES]
        avg = 0.5 * (jnp.exp2(z - r) + jnp.exp2(z - c_ref[:, o:o + LANES]))
        if diagonal:
            ri = lax.broadcasted_iota(jnp.int32, avg.shape, 0)
            ci = lax.broadcasted_iota(jnp.int32, avg.shape, 1) + o
            avg = avg - jnp.where(ri == ci, 1.0, 0.0)
        parts.append(avg.astype(BF16))
    return jnp.concatenate(parts, 1)


def far_text_kernel(scale, row, col, s, yx, w_ref, g_ref):
    rows = yx.shape[0] // 2
    r = spread(row[...])
    for k in (1, 0):
        w = weights_of(s, r, col, k, rows)
        w_ref[:, k * rows:(k + 1) * rows] = w
        g = lax.dot_general(w, yx[...], TN, preferred_element_type=F32)
        g_ref[k * rows:(k + 1) * rows, :] = (scale[0] * g).astype(g_ref.dtype)


def own_text_kernel(scale, row, col, si_in, sx_in, a_in, yx, w_ref, send_ref, keep_ref, s, a, sems):
    rows = a.shape[0]
    sources, targets = [a_in], [a]
    for k in (2, 3, 0, 1):
        cols = slice(k * rows, (k + 1) * rows)
        sources += [si_in.at[:, cols], sx_in.at[:, cols]]
        targets += [s.at[:rows, cols], s.at[rows:, cols]]
    copies = fetch(sources, targets, sems)
    r = spread(row[...])
    for i, k in enumerate((2, 3, 0, 1)):
        copies[1 + 2 * i].wait()
        copies[2 + 2 * i].wait()
        w = weights_of(s, r, col, k, rows, k == 0)
        w_ref[:, k * rows:(k + 1) * rows] = w
        if i == 0:
            copies[0].wait()
        g = lax.dot_general(w[:rows], a[...], TN, preferred_element_type=F32)
        g = scale[0] * (g + lax.dot_general(w[rows:], yx[rows:, :], TN, preferred_element_type=F32))
        if k >= 2:
            send_ref[(k - 2) * rows:(k - 1) * rows, :] = g.astype(send_ref.dtype)
        else:
            keep_ref[k * rows:(k + 1) * rows, :] = g


def y_grads_kernel(scale, wa, wb, va, vb, g_ref, send_ref):
    rows = wa.shape[0] // 2
    g = jnp.dot(wa[:rows, :], va[...], preferred_element_type=F32)
    g = scale[0] * (g + jnp.dot(wb[:rows, :], vb[...], preferred_element_type=F32))
    g_ref[...] = g
    send_ref[...] = g.astype(BF16)


def image_kernel(order, even, scale, w, t_in, wa, wb, va, vb, gy, gi_ref, gx_ref, t, sems):
    rows = t.shape[1]
    copies = fetch([quarter(order, t_in, k, rows) for k in range(4)], [t.at[k] for k in range(4)], sems)
    step = 512
    for o in range(0, gi_ref.shape[1], step):
        cols = slice(o, o + step)
        gx = jnp.dot(wa[rows:, :], va[:, cols], preferred_element_type=F32)
        gx = gx + jnp.dot(wb[rows:, :], vb[:, cols], preferred_element_type=F32)
        gi = 0.0
        for k in range(4):
            if o == 0:
                copies[k].wait()
            tk = t[k, :, cols]
            wk = w[:, k * rows:(k + 1) * rows]
            gx = gx + jnp.dot(wk[rows:], tk, preferred_element_type=F32)
            gi = gi + jnp.dot(wk[:rows], tk, preferred_element_type=F32)
        gi_ref[:, cols] = scale[0] * gi + jnp.where(even[0] == 1, 0.0, gy[:, cols])
        gx_ref[:, cols] = (scale[0] * gx).astype(BF16)


def finish_kernel(keep, got_zero, home_0, across, g_i, x_got, y_got, loss_in, scale_in, text_out, image_out, loss_ref,
                  b0, b1, b2, b3, b4, out, sems, out_sems):
    rows, d = b0.shape
    span = d // 2
    parts = [slice(0, span), slice(span, d)]
    texts = [fetch([r.at[:, c] for r in (got_zero, home_0, across)], [b.at[:, c] for b in (b0, b1, b2)], sems.at[i])
             for i, c in enumerate(parts)]
    images = [fetch([r.at[:, c] for r in (x_got, y_got)], [b.at[:, c] for b in (b3, b4)], sems.at[2 + i])
              for i, c in enumerate(parts)]
    loss_ref[...] = jnp.sum(loss_in[...], axis=1, keepdims=True) * scale_in[0]
    stores = []
    for i, c in enumerate(parts):
        for copy in images[i]:
            copy.wait()
        out[0, :, c] = g_i[:, c] + b3[:, c].astype(F32) + b4[:, c].astype(F32)
        stores.append(pltpu.make_async_copy(out.at[0, :, c], image_out.at[:, c], out_sems.at[2 * i]))
        stores[-1].start()
        for copy in texts[i]:
            copy.wait()
        total = keep[:rows, c] + b0[:, c].astype(F32) + b1[:, c].astype(F32) + b2[:, c].astype(F32)
        out[1, :, c] = total
        stores.append(pltpu.make_async_copy(out.at[1, :, c], text_out.at[:, c], out_sems.at[2 * i + 1]))
        stores[-1].start()
    for store in stores:
        store.wait()


def lse2(*parts):
    top = parts[0]
    for p in parts[1:]:
        top = jnp.maximum(top, p)
    total = sum(jnp.exp2(p - top) for p in parts)
    return top + jnp.log2(total)


def tie(*values):
    return lax.optimization_barrier(values)


def per_device(image_emb, text_emb, logit_scale):
    rows, d = image_emb.shape
    blocks = lax.axis_size("blk")
    rep = lax.axis_index("rep")
    even = lax.axis_index("blk") % 2 == 0
    evens = even.astype(jnp.int32).reshape(1)
    order = jnp.stack([rep ^ m for m in ORDER]).astype(jnp.int32)
    x_route = [(i, (i - 1) % blocks if i % 2 == 0 else (i - 3) % blocks) for i in range(blocks)]
    y_route = [(i, (i - 4) % blocks) for i in range(0, blocks, 2)]
    v_route = [(i, i ^ 1) for i in range(blocks)]
    x_back = [(b, a) for a, b in x_route]
    y_back = [(b, a) for a, b in y_route]
    tile = 2 * rows * rows * d

    def hop(value, route):
        return lax.ppermute(value, "blk", route)

    def swap(value, mask):
        return lax.ppermute(value, "rep", [(i, i ^ mask) for i in range(4)])

    def sems(n):
        return pltpu.SemaphoreType.DMA((n,))

    image_buf = pltpu.VMEM((rows, d), BF16)

    half = jnp.concatenate([lax.dynamic_slice_in_dim(text_emb, (rep ^ m) * rows, rows, 0) for m in ORDER[:2]])
    half, images = tie(half, image_emb)
    va = hop(half, v_route)
    x = hop(images, x_route)
    y = hop(images, y_route)
    wide, narrow = (1, 4 * rows), (1, rows)
    text_buf = pltpu.VMEM((4, rows, d), BF16)
    logits_buf = pltpu.VMEM((rows, 4 * rows), F32)

    logits_i, r_i, col_i, diag = local_call(
        own_image_kernel, "own_image", [SMEM] * 2 + [HBM] * 2,
        [((rows, 4 * rows), F32), (narrow, F32), (wide, F32), (narrow, F32)], 4 * tile,
        [image_buf, text_buf, logits_buf, sems(5), sems(4)], [HBM, VMEM, VMEM, VMEM],
    )(order, logit_scale, image_emb, text_emb)
    x, logits_i = tie(x, logits_i)
    logits_x, r_xt, col_x = local_call(
        x_logits_kernel, "x_logits", [SMEM] * 2 + [HBM] * 2,
        [((rows, 4 * rows), F32), (narrow, F32), (wide, F32)], 4 * tile,
        [image_buf, text_buf, logits_buf, sems(5), sems(4)], [HBM, VMEM, VMEM],
    )(order, logit_scale, x, text_emb)
    h_y = hop(r_i, y_route)
    va, y, r_xt, logits_x, h_y = tie(va, y, r_xt, logits_x, h_y)
    vb = swap(va, 1)
    s_a, row_a, col_a, yx, near_a = local_call(
        first_logits_kernel, "first_logits", [SMEM] * 2 + [HBM] * 4,
        [((2 * rows, 2 * rows), F32), ((1, 2 * rows), F32), ((1, 2 * rows), F32)] + [((2 * rows, d), BF16)] * 2, 4 * tile,
        [sems(4)],
    )(evens, logit_scale, image_emb, y, x, va)
    s_b, row_v, col_b, near_b = local_call(
        far_logits_kernel, "far_logits", [SMEM, VMEM, VMEM, HBM],
        [((2 * rows, 2 * rows), F32), ((1, 2 * rows), F32), ((1, 2 * rows), F32), ((2 * rows, d), BF16)], 4 * tile,
        [sems(2)],
    )(logit_scale, row_a, yx, vb)

    r_y, r_xv = row_v[:, :rows], row_v[:, rows:]
    r_x = lse2(r_xt, r_xv)
    h_i = jnp.where(even, r_i, lse2(r_i, r_y))
    col_t = lse2(col_i, col_x)
    col_v = jnp.concatenate([col_a, col_b], 1)
    blank = jnp.zeros((1, 3 * rows), F32)
    peer = hop(jnp.concatenate([col_v, col_t, jnp.concatenate([diag, blank], 1)]), v_route)
    down = hop(jnp.concatenate([h_i, r_x], 1), x_route)
    up = hop(jnp.concatenate([r_x, r_y], 1), x_back)
    y_i = hop(r_y, y_back)
    peer, down, up, y_i = tie(peer, down, up, y_i)
    h_x, x_y = down[:, :rows], down[:, rows:]
    x_i, y_x = up[:, :rows], up[:, rows:]
    row_x = jnp.where(even, lse2(h_x, r_x), lse2(h_x, r_x, y_x))
    row_i = jnp.where(even, lse2(r_i, x_i, y_i), lse2(h_i, x_i))
    row_y = jnp.where(even, lse2(r_y, h_y, x_y), row_i)
    row_yx = jnp.concatenate([row_y, row_x], 1)
    row_ix = jnp.concatenate([row_i, row_x], 1)
    pair = row_i + row_x - 2.0 * (diag + peer[2:, :rows])
    columns = jnp.concatenate([lse2(col_t, peer[:1]), lse2(col_v, peer[1:2])])
    stats = jnp.concatenate([columns, jnp.concatenate([pair, blank], 1)])
    got = [swap(stats, mask) for mask in (1, 2, 3)]
    aligned = [columns]
    for mask, g in zip((1, 2, 3), got):
        places = [PLACE[ORDER[k] ^ mask] for k in range(4)]
        aligned.append(jnp.concatenate([g[:2, p * rows:(p + 1) * rows] for p in places], 1))
    columns = lse2(*aligned)
    c_t, c_v = columns[:1], columns[1:]
    pair = sum((g[2:, :rows] for g in got), pair)
    column_sum = c_t + c_v
    loss_part = LN2 * sum((column_sum[:, k * rows:(k + 1) * rows] for k in range(4)), pair)

    def far_text(s, cols, dtype):
        return local_call(
            far_text_kernel, "far_text", [SMEM] + [VMEM] * 4,
            [((2 * rows, 2 * rows), BF16), ((2 * rows, d), dtype)], 4 * tile,
        )(logit_scale, row_yx, cols, s, yx)

    def shifted(value, xor, distance):
        span = blocks // 2

        def source(i):
            i = i ^ xor
            return (i + 4 * distance) % span + i // span * span
        return hop(value, [(source(i), i) for i in range(blocks)])

    w_t, send_t, keep_t = local_call(
        own_text_kernel, "own_text", [SMEM] + [VMEM] * 2 + [HBM] * 3 + [VMEM],
        [((2 * rows, 4 * rows), BF16), ((2 * rows, d), CORE), ((2 * rows, d), F32)], 8 * tile,
        [pltpu.VMEM((2 * rows, 4 * rows), F32), image_buf, sems(9)],
    )(logit_scale, row_ix, c_t, logits_i, logits_x, image_emb, yx)
    got_t = swap(send_t, 1)
    send_t, s_b = tie(send_t, s_b)
    w_b, send_v = far_text(s_b, c_v[:, 2 * rows:], CORE_V)
    send_v, s_a = tie(send_v, s_a)
    got_v = swap(send_v, 1)
    got = shifted(loss_part, 2, 0)
    w_a, keep_v = far_text(s_a, c_v[:, :2 * rows], F32)
    keep_v, got_v, got, got_t = tie(keep_v, got_v, got, got_t)
    loss_part = loss_part + got
    v_one = (keep_v[rows:] + got_v[rows:].astype(F32)).astype(BF16)
    v_zero = (keep_v[:rows] + got_v[:rows].astype(F32)).astype(BF16)
    v_one, v_zero, loss_part, w_a = tie(v_one, v_zero, loss_part, w_a)
    home_1 = hop(v_one, v_route)
    home_0 = hop(v_zero, v_route)
    g_y, g_y_send = local_call(
        y_grads_kernel, "y_grads", [SMEM] + [VMEM] * 4, [((rows, d), F32), ((rows, d), BF16)], 4 * tile,
    )(logit_scale, w_a, w_b, near_a, near_b)
    y_got = hop(g_y_send, y_back)
    g_i, g_x = local_call(
        image_kernel, "image_grads", [SMEM] * 3 + [VMEM, HBM] + [VMEM] * 5,
        [((rows, d), F32), ((rows, d), BF16)], 16 * tile, [text_buf, sems(4)],
    )(order, evens, logit_scale, w_t, text_emb, w_a, w_b, near_a, near_b, g_y)
    g_x, loss_part = tie(g_x, loss_part)
    got = [shifted(loss_part, 0, z) for z in (1, 2, 3)]
    got_zero = got_t[:rows]
    part = keep_t[rows:] + got_t[rows:].astype(F32)
    part, home_1, g_i, y_got, *got = tie(part, home_1, g_i, y_got, *got)
    loss_part = sum(got, loss_part)
    one = (part + home_1.astype(F32)).astype(BF16)
    one, loss_part, g_x = tie(one, loss_part, g_x)
    across = swap(one, 2)
    x_got = hop(g_x, x_back)
    got = [shifted(loss_part, x, z) for x, z in ((blocks // 2, 0), (0, 4), (blocks // 2, 4))]
    across, home_0, x_got, *got = tie(across, home_0, x_got, *got)
    grad_text, grad_image, loss = local_call(
        finish_kernel, "finish", [VMEM, ANY, ANY, ANY, VMEM, ANY, ANY, VMEM, SMEM],
        [((rows, d), F32), ((rows, d), F32), ((1, 1), F32)], tile,
        [image_buf] * 5 + [pltpu.VMEM((2, rows, d), F32), pltpu.SemaphoreType.DMA((4, 3)), sems(4)], [ANY, ANY, VMEM],
    )(keep_t, got_zero, home_0, across, g_i, x_got, y_got, sum(got, loss_part),
      jnp.full((1,), 1.0 / (2.0 * rows * blocks * 4), F32))
    return grad_image, grad_text, loss.reshape(1)


def solution(mesh):
    placed = (P(("blk", "rep"), None), P("blk", None), P())
    return jax.shard_map(
        per_device,
        mesh=mesh,
        in_specs=placed,
        out_specs=(P(("blk", "rep"), None), P(("blk", "rep"), None), P()),
        check_vma=False,
    )
```
